32 devices in a mesh: group: 2 (over y), tm: 4 (over z), mode: 2 (over x), col: 2 (over core).
Axes of the slice: x: 2, y: 2, z: 4, core: 2. Of those that a mesh axis runs over, the one named last changes fastest.
Arguments:
- flags: int32 [32], P(('group', 'tm')), parts along dimension 0, may hold values 0 or 1
- base_load: bfloat16 [32, 32, 1024], P(('group', 'tm'), 'col', 'mode'), parts along dimension 0, may hold values from -0.29882812 to 0.29882812
- solar_load: bfloat16 [64, 1024], P(('group', 'col'), 'mode'), parts along dimension 0, may hold values from -0.29882812 to 0.29882812
- target: bfloat16 [32, 32, 1024], P(('group', 'tm'), 'col', 'mode'), parts along dimension 0, may hold values from -6 to 6
- coarse_state: float32 [8, 32, 1024], P(('group', 'tm'), 'col', 'mode'), parts along dimension 0, may hold values from -6 to 6
- adjoint_state: float32 [8, 32, 1024], P(('group', 'tm'), 'col', 'mode'), parts along dimension 0, may hold values from -6 to 6
- step_sun: bfloat16 [1024, 1024], P('mode'), may hold values from -1 to 1
- step_eclipse: bfloat16 [1024, 1024], P('mode'), may hold values from -1 to 1
- coarse_step: bfloat16 [1024, 1024], P('mode'), may hold values from -1 to 1
Outputs:
- trajectory: float32 [32, 32, 1024], P(('group', 'tm'), 'col', 'mode'), parts along dimension 0
- adjoint_path: float32 [32, 32, 1024], P(('group', 'tm'), 'col', 'mode'), parts along dimension 0
The draws below stay inside these ranges and needn't reach their ends.
There are 2 independent parts, one for each index of `group`. The reference program is written for one: setup_inputs(seed, part) draws one part's arguments, and reference() takes and returns one part's arrays. A program takes and returns all parts, laid end to end along the dimension named above; an argument that names none is the same for every part. Nothing has to cross between parts.
All inputs are finite; a program needn't handle non-finite values. No bound on the sum of `flags` on one device may be relied on, other than what follows from the above.
Results may differ from the reference program's by a relative error of at most 0.0026.
Values may be sent and summed in bfloat16 or wider, within the bound.
A program may use at most 64 MiB of HBM per device.

```python
import math
import jax
import jax.numpy as jnp
from jax import lax

M = 1024
CF = 4
NC = 4
NT = 16
COLS = 32


def spectrum(key, lowest, highest, strength):
    base = jax.random.fold_in(key, 31)
    rate_key, noise_key, shade_key = jax.random.split(base, 3)
    place = jax.random.uniform(rate_key, (M,), jnp.float32)
    rates = jnp.exp(math.log(lowest) + place * (math.log(highest) - math.log(lowest)))
    keep = jnp.exp(-rates)
    coupling = jax.random.normal(noise_key, (M, M), jnp.float32) * (strength / math.sqrt(M))
    shade = jax.random.uniform(shade_key, (M,), jnp.float32, 0.5, 0.8)
    return (keep, coupling, shade)


def draw_step_sun(key, part):
    keep, coupling, shade = spectrum(key, 0.35, 1.0, 0.13)
    return (jnp.diag(keep) + coupling).astype(jnp.bfloat16)


def draw_step_eclipse(key, part):
    keep, coupling, shade = spectrum(key, 0.35, 1.0, 0.13)
    return (jnp.diag(keep * shade) + coupling).astype(jnp.bfloat16)


def draw_coarse_step(key, part):
    keep, coupling, shade = spectrum(key, 0.1, 0.7, 0.045)
    return (jnp.diag(keep) + coupling).astype(jnp.bfloat16)


def touch_ends(values, stream_key, least, high):
    longest = values.shape.index(max(values.shape))
    spots = []
    for shift in (0, 1):
        where = [jax.random.randint(jax.random.fold_in(stream_key, axis), (), 0, length) for axis, length in enumerate(values.shape)]
        where[longest] = (where[longest] + shift) % values.shape[longest]
        spots.append(tuple(where))
    return values.at[spots[0]].set(least).at[spots[1]].set(high)


def block_scale(own_key, shape, cuts, smallest, high):
    gain = 1.0
    for dim, blocks in cuts:
        draws = jax.random.uniform(jax.random.fold_in(jax.random.fold_in(own_key, 6), dim), (blocks,), jnp.float32, smallest / len(cuts), high / len(cuts))
        gain = gain * jnp.repeat(jnp.exp(draws), shape[dim] // blocks).reshape((-1,) + (1,) * (len(shape) - 1 - dim))
    return gain


def scatter_about(stream_key, extent, deviation, bound, shards=(), held_as=jnp.bfloat16):
    result = jax.random.normal(stream_key, extent, jnp.float32) * deviation
    if len(shards) > 0:
        result = block_scale(stream_key, extent, shards, -0.22, 0.18) * result
    return jnp.clip(result, min=-bound, max=bound).astype(held_as)


def setup_inputs(seed: int = 0, part: int = 0) -> dict:
    arg_keys = jax.random.split(jax.random.key(seed), 10)
    own_keys = jax.random.split(jax.random.fold_in(arg_keys[9], part), 10)
    flags = touch_ends((jax.random.randint(own_keys[0], (NT,), 0, 4) < 1).astype(jnp.int32), jax.random.fold_in(own_keys[0], 1), 0, 1)
    base_load = scatter_about(own_keys[1], (NT, COLS, M), 0.05, 0.29882812, ((0, 4), (1, 2), (2, 2)))
    solar_load = scatter_about(own_keys[2], (COLS, M), 0.05, 0.29882812, ((0, 2), (1, 2)))
    target = scatter_about(own_keys[3], (NT, COLS, M), 1.0, 6.0, ((0, 4), (1, 2), (2, 2)))
    coarse_state = scatter_about(own_keys[4], (NC, COLS, M), 1.0, 6.0, ((0, 4), (1, 2), (2, 2)), jnp.float32)
    adjoint_state = scatter_about(own_keys[5], (NC, COLS, M), 1.0, 6.0, ((0, 4), (1, 2), (2, 2)), jnp.float32)
    step_sun = draw_step_sun(jax.random.fold_in(arg_keys[9], 71), part)
    step_eclipse = draw_step_eclipse(jax.random.fold_in(arg_keys[9], 71), part)
    coarse_step = draw_coarse_step(jax.random.fold_in(arg_keys[9], 71), part)
    return dict(flags=flags, base_load=base_load, solar_load=solar_load, target=target, coarse_state=coarse_state, adjoint_state=adjoint_state, step_sun=step_sun, step_eclipse=step_eclipse, coarse_step=coarse_step)


OBJ_WEIGHT = 0.0625
EXACT = lax.Precision.HIGHEST


def forward_interval(start, grid_flags, grid_force, step_sun, step_eclipse, count):
    current = start
    results = []
    for m in range(count):
        matrix = jnp.where(grid_flags[m] == 1, step_eclipse, step_sun)
        current = jnp.dot(current.astype(jnp.bfloat16), matrix.T, preferred_element_type=jnp.float32) + grid_force[m]
        results.append(current)
    return jnp.stack(results)


def backward_interval(start, grid_flags, grid_source, step_sun, step_eclipse, count):
    current = start
    results = {}
    for m in range(CF - 1, CF - 1 - count, -1):
        matrix = jnp.where(grid_flags[m] == 1, step_eclipse, step_sun)
        current = jnp.dot(current.astype(jnp.bfloat16), matrix, preferred_element_type=jnp.float32) + grid_source[m]
        results[m] = current
    return jnp.stack([results[m] for m in sorted(results)])


def reference(flags, base_load, solar_load, target, coarse_state, adjoint_state, step_sun, step_eclipse, coarse_step):
    intervals = coarse_state.shape[0]
    columns = coarse_state.shape[1]
    modes = coarse_state.shape[2]
    grid_flags = flags.reshape(intervals, CF)
    sun_on = (1 - grid_flags).astype(jnp.float32)
    force = base_load.astype(jnp.float32).reshape(intervals, CF, columns, modes) + sun_on[:, :, None, None] * solar_load.astype(jnp.float32)[None, None]
    coarse_full = coarse_step.astype(jnp.float32)

    def forward_runner(count):
        def runner(item):
            start, flag_row, force_row = item
            return forward_interval(start, flag_row, force_row, step_sun, step_eclipse, count)
        return runner

    ends = lax.map(forward_runner(CF), (coarse_state, grid_flags, force))[:, CF - 1]
    zero_block = jnp.zeros((1, columns, modes), jnp.float32)
    residual = jnp.concatenate([zero_block, ends[:-1] - coarse_state[1:]], 0)

    def primal_coarse(carry, resid):
        fresh = jnp.dot(carry, coarse_full.T, precision=EXACT) + resid
        return fresh, fresh

    _, correction = lax.scan(primal_coarse, jnp.zeros((columns, modes), jnp.float32), residual)
    corrected = coarse_state + correction
    inner = lax.map(forward_runner(CF - 1), (corrected, grid_flags, force))
    trajectory = jnp.concatenate([corrected[:, None], inner], 1).reshape(intervals * CF, columns, modes)

    source = OBJ_WEIGHT * (trajectory - target.astype(jnp.float32))
    grid_source = source.reshape(intervals, CF, columns, modes)

    def backward_runner(count):
        def runner(item):
            start, flag_row, source_row = item
            return backward_interval(start, flag_row, source_row, step_sun, step_eclipse, count)
        return runner

    starts = jnp.concatenate([adjoint_state[1:], zero_block], 0)
    back_ends = lax.map(backward_runner(CF), (starts, grid_flags, grid_source))[:, 0]
    back_residual = back_ends - adjoint_state

    def adjoint_coarse(carry, resid):
        fresh = jnp.dot(carry, coarse_full, precision=EXACT) + resid
        return fresh, fresh

    _, back_correction = lax.scan(adjoint_coarse, jnp.zeros((columns, modes), jnp.float32), back_residual, reverse=True)
    back_corrected = adjoint_state + back_correction
    restarts = jnp.concatenate([back_corrected[1:], zero_block], 0)
    back_inner = lax.map(backward_runner(CF - 1), (restarts, grid_flags, grid_source))
    adjoint_path = jnp.concatenate([back_corrected[:, None], back_inner], 1).reshape(intervals * CF, columns, modes)
    return trajectory, adjoint_path
```

```python
import functools

import jax
import jax.numpy as jnp
from jax import lax
from jax.experimental import pallas as pl
from jax.experimental.pallas import tpu as pltpu
from jax.sharding import PartitionSpec as P

OBJ_WEIGHT = 0.0625
MESH = pl.DeviceIdType.MESH
BF16 = jnp.bfloat16
F32 = jnp.float32
TILE = 256
NT_DIMS = (((1,), (1,)), ((), ()))
NN_DIMS = (((1,), (0,)), ((), ()))


def remote(src, dst, send, recv, **where):
    return pltpu.make_async_remote_copy(
        src_ref=src, dst_ref=dst, send_sem=send, recv_sem=recv, device_id=where, device_id_type=MESH
    )


def times_transposed(rows, tile_of, modes):
    parts = []
    for j in range(modes // TILE):
        tile = tile_of(pl.ds(j * TILE, TILE), slice(None))
        parts.append(lax.dot_general(rows, tile, NT_DIMS, preferred_element_type=F32))
    return jnp.concatenate(parts, axis=1)


def times_plain(rows, tile_of, modes):
    parts = []
    for j in range(modes // TILE):
        tile = tile_of(slice(None), pl.ds(j * TILE, TILE))
        parts.append(lax.dot_general(rows, tile, NN_DIMS, preferred_element_type=F32))
    return jnp.concatenate(parts, axis=1)


def pieces(value):
    hi = value.astype(BF16)
    rest = value - hi.astype(F32)
    mid = rest.astype(BF16)
    lo = (rest - mid.astype(F32)).astype(BF16)
    return jnp.concatenate([hi, mid, lo], axis=0)


def collect(product, cols):
    return product[:cols] + product[cols : 2 * cols] + product[2 * cols :]


def kernel(
    modes_n,
    times_n,
    chunks,
    flags,
    base,
    solar,
    target,
    state,
    adjoint,
    sun,
    eclipse,
    coarse,
    traj_out,
    path_out,
    mats,
    cmat,
    base_f,
    solar_f,
    target_f,
    state_f,
    adj_f,
    state_next,
    adj_next,
    traj,
    path,
    res_f,
    res_b,
    corr,
    own_sem,
    small_send,
    small_recv,
    next_send,
    next_recv,
    one_send,
    one_recv,
    y_send,
    y_recv,
    c_send,
    c_recv,
    d_send,
    d_recv,
    rf_send,
    rf_recv,
    rb_send,
    rb_recv,
):
    g = lax.axis_index("group")
    t = lax.axis_index("tm")
    m = lax.axis_index("mode")
    c = lax.axis_index("col")
    rows = sun.shape[0]
    modes = sun.shape[1]
    steps, cols = base.shape[0], base.shape[1]
    quarter = rows // 4
    piece = quarter // chunks
    mate = 1 - c
    twin = 1 - g

    def lanes(index):
        return pl.ds(pl.multiple_of(index * rows, 128), rows)

    mine = lanes(m)

    own = [
        (state.at[0], state_f.at[:, mine]),
        (base, base_f.at[:, :, mine]),
        (solar, solar_f.at[:, mine]),
        (sun, mats.at[0, pl.ds(pl.multiple_of(m * rows, 16), rows), :]),
        (eclipse, mats.at[1, pl.ds(pl.multiple_of(m * rows, 16), rows), :]),
        (target, target_f.at[:, :, mine]),
        (adjoint.at[0], adj_f.at[:, mine]),
        (coarse, cmat.at[pl.ds(pl.multiple_of(m * rows, 16), rows), :]),
    ]
    own_copies = [pltpu.make_async_copy(s, d, own_sem.at[i]) for i, (s, d) in enumerate(own)]
    for copy in own_copies:
        copy.start()

    barrier = pltpu.get_barrier_semaphore()
    pl.semaphore_signal(barrier, inc=1, device_id={"col": mate}, device_id_type=MESH)
    pl.semaphore_signal(barrier, inc=1, device_id={"group": twin}, device_id_type=MESH)
    for d in range(1, modes_n):
        pl.semaphore_signal(barrier, inc=1, device_id={"mode": lax.rem(m + d, modes_n)}, device_id_type=MESH)
    for d in range(1, times_n):
        pl.semaphore_signal(barrier, inc=1, device_id={"tm": lax.rem(t + d, times_n)}, device_id_type=MESH)
    pl.semaphore_wait(barrier, modes_n + times_n)

    def peer(d):
        return lax.rem(m + d, modes_n)

    def source(d):
        return lax.rem(m + modes_n - d, modes_n)

    small_srcs = [state.at[0], base, solar, target, adjoint.at[0]]

    def small_dst(kind, where):
        if kind == 0:
            return state_f.at[:, where]
        if kind == 1:
            return base_f.at[:, :, where]
        if kind == 2:
            return solar_f.at[:, where]
        if kind == 3:
            return target_f.at[:, :, where]
        return adj_f.at[:, where]

    def small(kind, d):
        at = kind * (modes_n - 1) + d - 1
        return remote(
            small_srcs[kind], small_dst(kind, mine), small_send.at[at], small_recv.at[at], mode=peer(d)
        )

    mat_srcs = [sun, eclipse, coarse]

    def mat_rows(k, start):
        where = pl.ds(pl.multiple_of(start, 16), piece)
        if k < 2:
            return mats.at[k, where, :]
        return cmat.at[where, :]

    order = []
    for k in range(3):
        for q in range(chunks):
            for d in range(1, modes_n):
                order.append((k, q, d))

    part = (g * 2 + c) * quarter
    twin_part = (twin * 2 + c) * quarter

    def first(at):
        k, q, d = order[at]
        inside = part + q * piece
        return remote(
            mat_srcs[k].at[pl.ds(pl.multiple_of(inside, 16), piece), :],
            mat_rows(k, m * rows + inside),
            one_send.at[at],
            one_recv.at[at],
            mode=peer(d),
        )

    def arrived_rows(at, owner_part):
        k, q, d = order[at]
        return mat_rows(k, source(d) * rows + owner_part + q * piece)

    def to_twin(at):
        ref = arrived_rows(at, part)
        return remote(ref, ref, y_send.at[at], y_recv.at[at], group=twin)

    def to_mate(at):
        ref = arrived_rows(at, part)
        return remote(ref, ref, c_send.at[at], c_recv.at[at], col=mate)

    def twin_to_mate(at):
        ref = arrived_rows(at, twin_part)
        return remote(ref, ref, d_send.at[at], d_recv.at[at], col=mate)

    per_mat = chunks * (modes_n - 1)

    def start_small(kinds):
        for kind in kinds:
            for d in range(1, modes_n):
                small(kind, d).start()

    start_small((0, 1, 2))
    for at in range(2 * per_mat):
        first(at).start()
    start_small((4, 3))
    for at in range(2 * per_mat, 3 * per_mat):
        first(at).start()

    def wait_small(kind):
        for d in range(1, modes_n):
            small(kind, d).wait_recv()

    back_down = lax.rem(t + times_n - 1, times_n)

    def next_copy(index):
        src, dst = ((state_f, state_next), (adj_f, adj_next))[index]
        return remote(src, dst, next_send.at[index], next_recv.at[index], tm=back_down)

    own_copies[0].wait()
    wait_small(0)

    @pl.when(t > 0)
    def _():
        next_copy(0).start()

    def relay(first_at, last_at):
        for at in range(first_at, last_at + 1):
            if at < last_at:
                first(at).wait_recv()
                to_twin(at).start()
                to_mate(at).start()
            if at > first_at:
                to_twin(at - 1).wait_recv()
                twin_to_mate(at - 1).start()

    def settle(first_at, last_at):
        for at in range(first_at, last_at):
            to_mate(at).wait_recv()
            twin_to_mate(at).wait_recv()

    relay(0, 2 * per_mat)
    for index in (1, 2, 3, 4):
        own_copies[index].wait()
    wait_small(1)
    wait_small(2)
    settle(0, 2 * per_mat)

    def forcing(n):
        sun_on = (1 - flags[n]).astype(F32)
        return base_f[n].astype(F32) + sun_on * solar_f[...].astype(F32)

    def forward(n, w):
        flag = flags[n]
        return times_transposed(w.astype(BF16), lambda a, b: mats[flag, a, b], modes) + forcing(n)

    ends = lax.fori_loop(0, steps, forward, state_f[...])

    @pl.when(t < times_n - 1)
    def _():
        next_copy(0).wait_recv()
        res_f[t + 1] = ends - state_next[...]

    def res_copy(k):
        slot = lax.rem(t + 1, times_n)
        return remote(
            res_f.at[slot], res_f.at[slot], rf_send.at[k - 1], rf_recv.at[slot], tm=lax.rem(t + k, times_n)
        )

    for k in range(times_n - 1, 0, -1):

        @pl.when(t + k < times_n)
        def _():
            res_copy(k).start()

    own_copies[6].wait()
    wait_small(4)

    @pl.when(t > 0)
    def _():
        next_copy(1).start()

    relay(2 * per_mat, 3 * per_mat)
    own_copies[5].wait()
    own_copies[7].wait()
    wait_small(3)
    settle(2 * per_mat, 3 * per_mat)

    def wait_res(j):
        remote(res_f.at[j], res_f.at[j], rf_send.at[0], rf_recv.at[j], tm=t).wait_recv()

    corr[...] = jnp.zeros_like(corr)

    @pl.when(t >= 1)
    def _():
        wait_res(1)
        corr[...] = res_f[1]

    def coarse_up(j, carry):
        wait_res(j)
        product = times_transposed(pieces(corr[...]), lambda a, b: cmat[a, b], modes)
        corr[...] = collect(product, cols) + res_f[j]
        return carry

    lax.fori_loop(2, t + 1, coarse_up, 0)

    corrected = state_f[...] + corr[...]
    traj[0] = corrected

    def forward_keep(n, w):
        w = forward(n, w)
        traj[n + 1] = w
        return w

    lax.fori_loop(0, steps - 1, forward_keep, corrected)

    def backward(n, w):
        flag = flags[n]
        product = times_plain(w.astype(BF16), lambda a, b: mats[flag, a, b], modes)
        return product + OBJ_WEIGHT * (traj[n] - target_f[n].astype(F32))

    @pl.when(t < times_n - 1)
    def _():
        next_copy(1).wait_recv()

    @pl.when(t == times_n - 1)
    def _():
        adj_next[...] = jnp.zeros_like(adj_next)

    back = lax.fori_loop(0, steps, lambda i, w: backward(steps - 1 - i, w), adj_next[...])
    res_b[t] = back - adj_f[...]

    def back_copy(k):
        return remote(res_b.at[t], res_b.at[t], rb_send.at[k - 1], rb_recv.at[t], tm=lax.rem(t + times_n - k, times_n))

    for k in range(times_n - 1, 0, -1):

        @pl.when(t - k >= 0)
        def _():
            back_copy(k).start()

    traj_out[...] = traj[:, :, mine]

    def wait_back(j):
        remote(res_b.at[j], res_b.at[j], rb_send.at[0], rb_recv.at[j], tm=t).wait_recv()

    @pl.when(t < times_n - 1)
    def _():
        wait_back(times_n - 1)

    corr[...] = res_b[times_n - 1]

    def coarse_down(i, carry):
        j = times_n - 2 - i
        wait_back(j)
        product = times_plain(pieces(corr[...]), lambda a, b: cmat[a, b], modes)
        corr[...] = collect(product, cols) + res_b[j]
        return carry

    lax.fori_loop(0, times_n - 2 - t, coarse_down, 0)

    @pl.when(t < times_n - 1)
    def _():
        later = corr[...]
        adj_next[...] = adj_next[...] + later
        product = times_plain(pieces(later), lambda a, b: cmat[a, b], modes)
        corr[...] = collect(product, cols) + res_b[t]

    path[0] = adj_f[...] + corr[...]

    def backward_keep(i, w):
        n = steps - 1 - i
        w = backward(n, w)
        path[n] = w
        return w

    lax.fori_loop(0, steps - 1, backward_keep, adj_next[...])
    path_out[...] = path[:, :, mine]

    for kind in range(5):
        for d in range(1, modes_n):
            small(kind, d).wait_send()
    for at in range(3 * per_mat):
        first(at).wait_send()
        to_twin(at).wait_send()
        to_mate(at).wait_send()
        twin_to_mate(at).wait_send()

    @pl.when(t > 0)
    def _():
        next_copy(0).wait_send()
        next_copy(1).wait_send()

    for k in range(times_n - 1, 0, -1):

        @pl.when(t + k < times_n)
        def _():
            res_copy(k).wait_send()

        @pl.when(t - k >= 0)
        def _():
            back_copy(k).wait_send()


def local(modes_n, times_n, flags, base, solar, target, state, adjoint, sun, eclipse, coarse):
    rows, modes = sun.shape
    steps, cols = base.shape[0], base.shape[1]
    chunks = max(1, min(4, rows // 4 // 32))
    count = 3 * chunks * (modes_n - 1)
    dma = pltpu.SemaphoreType.DMA
    hbm = pl.BlockSpec(memory_space=pl.ANY)
    vmem = pl.BlockSpec(memory_space=pltpu.VMEM)
    outs = jax.ShapeDtypeStruct((steps, cols, rows), F32)
    return pl.pallas_call(
        functools.partial(kernel, modes_n, times_n, chunks),
        out_shape=(outs, outs),
        in_specs=[pl.BlockSpec(memory_space=pltpu.SMEM)] + [hbm] * 8,
        out_specs=(vmem, vmem),
        scratch_shapes=[
            pltpu.VMEM((2, modes, modes), BF16),
            pltpu.VMEM((modes, modes), BF16),
            pltpu.VMEM((steps, cols, modes), BF16),
            pltpu.VMEM((cols, modes), BF16),
            pltpu.VMEM((steps, cols, modes), BF16),
            pltpu.VMEM((cols, modes), F32),
            pltpu.VMEM((cols, modes), F32),
            pltpu.VMEM((cols, modes), F32),
            pltpu.VMEM((cols, modes), F32),
            pltpu.VMEM((steps, cols, modes), F32),
            pltpu.VMEM((steps, cols, modes), F32),
            pltpu.VMEM((times_n, cols, modes), F32),
            pltpu.VMEM((times_n, cols, modes), F32),
            pltpu.VMEM((cols, modes), F32),
            dma((8,)),
            dma((5 * (modes_n - 1),)),
            dma((5 * (modes_n - 1),)),
            dma((2,)),
            dma((2,)),
            dma((count,)),
            dma((count,)),
            dma((count,)),
            dma((count,)),
            dma((count,)),
            dma((count,)),
            dma((count,)),
            dma((count,)),
            dma((times_n - 1,)),
            dma((times_n,)),
            dma((times_n - 1,)),
            dma((times_n,)),
        ],
        compiler_params=pltpu.CompilerParams(
            collective_id=0, has_side_effects=True, vmem_limit_bytes=32 * 1024 * 1024
        ),
    )(flags, base, solar, target, state, adjoint, sun, eclipse, coarse)


def solution(mesh):
    cells = P(("group", "tm"), "col", "mode")
    in_specs = (
        P(("group", "tm")),
        cells,
        P(("group", "col"), "mode"),
        cells,
        cells,
        cells,
        P("mode", None),
        P("mode", None),
        P("mode", None),
    )
    call = functools.partial(local, mesh.shape["mode"], mesh.shape["tm"])
    return jax.shard_map(call, mesh=mesh, in_specs=in_specs, out_specs=(cells, cells), check_vma=False)
```

```python
import functools

import jax
import jax.numpy as jnp
from jax import lax
from jax.experimental import pallas as pl
from jax.experimental.pallas import tpu as pltpu
from jax.sharding import PartitionSpec as P

OBJ_WEIGHT = 0.0625
MESH = pl.DeviceIdType.MESH
BF16 = jnp.bfloat16
F32 = jnp.float32
TILE = 256
NT_DIMS = (((1,), (1,)), ((), ()))
NN_DIMS = (((1,), (0,)), ((), ()))


def remote(src, dst, send, recv, **where):
    return pltpu.make_async_remote_copy(
        src_ref=src, dst_ref=dst, send_sem=send, recv_sem=recv, device_id=where, device_id_type=MESH
    )


def times_transposed(rows, tile_of, modes):
    parts = []
    for j in range(modes // TILE):
        tile = tile_of(pl.ds(j * TILE, TILE), slice(None))
        parts.append(lax.dot_general(rows, tile, NT_DIMS, preferred_element_type=F32))
    return jnp.concatenate(parts, axis=1)


def times_plain(rows, tile_of, modes):
    parts = []
    for j in range(modes // TILE):
        tile = tile_of(slice(None), pl.ds(j * TILE, TILE))
        parts.append(lax.dot_general(rows, tile, NN_DIMS, preferred_element_type=F32))
    return jnp.concatenate(parts, axis=1)


def pieces(value):
    hi = value.astype(BF16)
    rest = value - hi.astype(F32)
    mid = rest.astype(BF16)
    lo = (rest - mid.astype(F32)).astype(BF16)
    return jnp.concatenate([hi, mid, lo], axis=0)


def collect(product, cols):
    return product[:cols] + product[cols : 2 * cols] + product[2 * cols :]


def kernel(
    modes_n,
    times_n,
    chunks,
    flags,
    base,
    solar,
    target,
    state,
    adjoint,
    sun,
    eclipse,
    coarse,
    traj_out,
    path_out,
    mats,
    cmat,
    base_f,
    solar_f,
    target_f,
    state_f,
    adj_f,
    state_next,
    adj_next,
    traj,
    path,
    res_f,
    res_b,
    corr,
    own_sem,
    small_send,
    small_recv,
    next_send,
    next_recv,
    one_send,
    one_recv,
    y_send,
    y_recv,
    c_send,
    c_recv,
    d_send,
    d_recv,
    far_low,
    far_high,
    rf_send,
    rf_recv,
    rb_send,
    rb_recv,
):
    g = lax.axis_index("group")
    t = lax.axis_index("tm")
    m = lax.axis_index("mode")
    c = lax.axis_index("col")
    rows = sun.shape[0]
    modes = sun.shape[1]
    steps, cols = base.shape[0], base.shape[1]
    quarter = rows // 4
    piece = quarter // chunks
    mate = 1 - c
    twin = 1 - g

    def lanes(index):
        return pl.ds(pl.multiple_of(index * rows, 128), rows)

    mine = lanes(m)

    own = [
        (state.at[0], state_f.at[:, mine]),
        (base, base_f.at[:, :, mine]),
        (solar, solar_f.at[:, mine]),
        (sun, mats.at[0, pl.ds(pl.multiple_of(m * rows, 16), rows), :]),
        (eclipse, mats.at[1, pl.ds(pl.multiple_of(m * rows, 16), rows), :]),
        (target, target_f.at[:, :, mine]),
        (adjoint.at[0], adj_f.at[:, mine]),
        (coarse, cmat.at[pl.ds(pl.multiple_of(m * rows, 16), rows), :]),
    ]
    own_copies = [pltpu.make_async_copy(s, d, own_sem.at[i]) for i, (s, d) in enumerate(own)]
    for copy in own_copies:
        copy.start()

    barrier = pltpu.get_barrier_semaphore()
    pl.semaphore_signal(barrier, inc=1, device_id={"col": mate}, device_id_type=MESH)
    pl.semaphore_signal(barrier, inc=1, device_id={"group": twin}, device_id_type=MESH)
    for d in range(1, modes_n):
        pl.semaphore_signal(barrier, inc=1, device_id={"mode": lax.rem(m + d, modes_n)}, device_id_type=MESH)

    def signal_tm(semaphore, where):
        pl.semaphore_signal(semaphore, inc=1, device_id={"tm": where}, device_id_type=MESH)

    @pl.when(t > 0)
    def _():
        signal_tm(barrier, t - 1)

    @pl.when(t < times_n - 1)
    def _():
        signal_tm(barrier, t + 1)

    has_low = lax.div(t + times_n - 1, times_n)
    has_high = lax.div(2 * times_n - 2 - t, times_n)
    pl.semaphore_wait(barrier, modes_n + 1 + has_low + has_high)

    def pass_on(entry):
        @pl.when(jnp.logical_and(t - 1 - entry >= 0, t + 1 < times_n))
        def _():
            signal_tm(far_low.at[entry], t + 1)

        @pl.when(jnp.logical_and(t + 1 + entry < times_n, t - 1 >= 0))
        def _():
            signal_tm(far_high.at[entry], t - 1)

    def hear(entry):
        @pl.when(t - 2 - entry >= 0)
        def _():
            pl.semaphore_wait(far_low.at[entry], 1)

        @pl.when(t + 2 + entry < times_n)
        def _():
            pl.semaphore_wait(far_high.at[entry], 1)

    def peer(d):
        return lax.rem(m + d, modes_n)

    def source(d):
        return lax.rem(m + modes_n - d, modes_n)

    small_srcs = [state.at[0], base, solar, target, adjoint.at[0]]

    def small_dst(kind, where):
        if kind == 0:
            return state_f.at[:, where]
        if kind == 1:
            return base_f.at[:, :, where]
        if kind == 2:
            return solar_f.at[:, where]
        if kind == 3:
            return target_f.at[:, :, where]
        return adj_f.at[:, where]

    def small(kind, d):
        at = kind * (modes_n - 1) + d - 1
        return remote(
            small_srcs[kind], small_dst(kind, mine), small_send.at[at], small_recv.at[at], mode=peer(d)
        )

    mat_srcs = [sun, eclipse, coarse]

    def mat_rows(k, start):
        where = pl.ds(pl.multiple_of(start, 16), piece)
        if k < 2:
            return mats.at[k, where, :]
        return cmat.at[where, :]

    order = []
    for k in range(3):
        for q in range(chunks):
            for d in range(1, modes_n):
                order.append((k, q, d))

    part = (g * 2 + c) * quarter
    twin_part = (twin * 2 + c) * quarter

    def first(at):
        k, q, d = order[at]
        inside = part + q * piece
        return remote(
            mat_srcs[k].at[pl.ds(pl.multiple_of(inside, 16), piece), :],
            mat_rows(k, m * rows + inside),
            one_send.at[at],
            one_recv.at[at],
            mode=peer(d),
        )

    def arrived_rows(at, owner_part):
        k, q, d = order[at]
        return mat_rows(k, source(d) * rows + owner_part + q * piece)

    def to_twin(at):
        ref = arrived_rows(at, part)
        return remote(ref, ref, y_send.at[at], y_recv.at[at], group=twin)

    def to_mate(at):
        ref = arrived_rows(at, part)
        return remote(ref, ref, c_send.at[at], c_recv.at[at], col=mate)

    def twin_to_mate(at):
        ref = arrived_rows(at, twin_part)
        return remote(ref, ref, d_send.at[at], d_recv.at[at], col=mate)

    per_mat = chunks * (modes_n - 1)

    def start_small(kinds):
        for kind in kinds:
            for d in range(1, modes_n):
                small(kind, d).start()

    for at in range(2 * per_mat):
        first(at).start()
    start_small((0, 1, 2))
    start_small((4, 3))
    for at in range(2 * per_mat, 3 * per_mat):
        first(at).start()

    if times_n > 2:
        pass_on(0)

    def wait_small(kind):
        for d in range(1, modes_n):
            small(kind, d).wait_recv()

    back_down = lax.rem(t + times_n - 1, times_n)

    def next_copy(index):
        src, dst = ((state_f, state_next), (adj_f, adj_next))[index]
        return remote(src, dst, next_send.at[index], next_recv.at[index], tm=back_down)

    def relay(first_at, last_at):
        for at in range(first_at, last_at + 1):
            if at < last_at:
                first(at).wait_recv()
                to_twin(at).start()
                to_mate(at).start()
            if at > first_at:
                to_twin(at - 1).wait_recv()
                twin_to_mate(at - 1).start()

    def settle(first_at, last_at):
        for at in range(first_at, last_at):
            to_mate(at).wait_recv()
            twin_to_mate(at).wait_recv()

    relay(0, 2 * per_mat)
    own_copies[0].wait()
    wait_small(0)

    @pl.when(t > 0)
    def _():
        next_copy(0).start()

    for index in (1, 2, 3, 4):
        own_copies[index].wait()
    wait_small(1)
    wait_small(2)
    settle(0, 2 * per_mat)

    def forcing(n):
        sun_on = (1 - flags[n]).astype(F32)
        return base_f[n].astype(F32) + sun_on * solar_f[...].astype(F32)

    def forward(n, w):
        flag = flags[n]
        return times_transposed(w.astype(BF16), lambda a, b: mats[flag, a, b], modes) + forcing(n)

    ends = lax.fori_loop(0, steps, forward, state_f[...])

    @pl.when(t < times_n - 1)
    def _():
        next_copy(0).wait_recv()
        res_f[t + 1] = ends - state_next[...]

    for entry in range(times_n - 2):
        hear(entry)
        if entry + 1 < times_n - 2:
            pass_on(entry + 1)

    def res_copy(k):
        slot = lax.rem(t + 1, times_n)
        return remote(
            res_f.at[slot], res_f.at[slot], rf_send.at[k - 1], rf_recv.at[slot], tm=lax.rem(t + k, times_n)
        )

    for k in range(times_n - 1, 0, -1):

        @pl.when(t + k < times_n)
        def _():
            res_copy(k).start()

    own_copies[6].wait()
    wait_small(4)

    @pl.when(t > 0)
    def _():
        next_copy(1).start()

    relay(2 * per_mat, 3 * per_mat)
    own_copies[5].wait()
    own_copies[7].wait()
    wait_small(3)
    settle(2 * per_mat, 3 * per_mat)

    def wait_res(j):
        remote(res_f.at[j], res_f.at[j], rf_send.at[0], rf_recv.at[j], tm=t).wait_recv()

    corr[...] = jnp.zeros_like(corr)

    @pl.when(t >= 1)
    def _():
        wait_res(1)
        corr[...] = res_f[1]

    def coarse_up(j, carry):
        wait_res(j)
        product = times_transposed(pieces(corr[...]), lambda a, b: cmat[a, b], modes)
        corr[...] = collect(product, cols) + res_f[j]
        return carry

    lax.fori_loop(2, t + 1, coarse_up, 0)

    corrected = state_f[...] + corr[...]
    traj[0] = corrected

    def forward_keep(n, w):
        w = forward(n, w)
        traj[n + 1] = w
        return w

    lax.fori_loop(0, steps - 1, forward_keep, corrected)

    def backward(n, w):
        flag = flags[n]
        product = times_plain(w.astype(BF16), lambda a, b: mats[flag, a, b], modes)
        return product + OBJ_WEIGHT * (traj[n] - target_f[n].astype(F32))

    @pl.when(t < times_n - 1)
    def _():
        next_copy(1).wait_recv()

    @pl.when(t == times_n - 1)
    def _():
        adj_next[...] = jnp.zeros_like(adj_next)

    back = lax.fori_loop(0, steps, lambda i, w: backward(steps - 1 - i, w), adj_next[...])
    res_b[t] = back - adj_f[...]

    def back_copy(k):
        return remote(res_b.at[t], res_b.at[t], rb_send.at[k - 1], rb_recv.at[t], tm=lax.rem(t + times_n - k, times_n))

    for k in range(times_n - 1, 0, -1):

        @pl.when(t - k >= 0)
        def _():
            back_copy(k).start()

    traj_out[...] = traj[:, :, mine]

    def wait_back(j):
        remote(res_b.at[j], res_b.at[j], rb_send.at[0], rb_recv.at[j], tm=t).wait_recv()

    @pl.when(t < times_n - 1)
    def _():
        wait_back(times_n - 1)

    corr[...] = res_b[times_n - 1]

    def coarse_down(i, carry):
        j = times_n - 2 - i
        wait_back(j)
        product = times_plain(pieces(corr[...]), lambda a, b: cmat[a, b], modes)
        corr[...] = collect(product, cols) + res_b[j]
        return carry

    lax.fori_loop(0, times_n - 2 - t, coarse_down, 0)

    @pl.when(t < times_n - 1)
    def _():
        later = corr[...]
        adj_next[...] = adj_next[...] + later
        product = times_plain(pieces(later), lambda a, b: cmat[a, b], modes)
        corr[...] = collect(product, cols) + res_b[t]

    path[0] = adj_f[...] + corr[...]

    def backward_keep(i, w):
        n = steps - 1 - i
        w = backward(n, w)
        path[n] = w
        return w

    lax.fori_loop(0, steps - 1, backward_keep, adj_next[...])
    path_out[...] = path[:, :, mine]

    for kind in range(5):
        for d in range(1, modes_n):
            small(kind, d).wait_send()
    for at in range(3 * per_mat):
        first(at).wait_send()
        to_twin(at).wait_send()
        to_mate(at).wait_send()
        twin_to_mate(at).wait_send()

    @pl.when(t > 0)
    def _():
        next_copy(0).wait_send()
        next_copy(1).wait_send()

    for k in range(times_n - 1, 0, -1):

        @pl.when(t + k < times_n)
        def _():
            res_copy(k).wait_send()

        @pl.when(t - k >= 0)
        def _():
            back_copy(k).wait_send()


def local(modes_n, times_n, flags, base, solar, target, state, adjoint, sun, eclipse, coarse):
    rows, modes = sun.shape
    steps, cols = base.shape[0], base.shape[1]
    chunks = max(1, min(2, rows // 4 // 32))
    count = 3 * chunks * (modes_n - 1)
    dma = pltpu.SemaphoreType.DMA
    hbm = pl.BlockSpec(memory_space=pl.ANY)
    vmem = pl.BlockSpec(memory_space=pltpu.VMEM)
    outs = jax.ShapeDtypeStruct((steps, cols, rows), F32)
    return pl.pallas_call(
        functools.partial(kernel, modes_n, times_n, chunks),
        out_shape=(outs, outs),
        in_specs=[pl.BlockSpec(memory_space=pltpu.SMEM)] + [hbm] * 8,
        out_specs=(vmem, vmem),
        scratch_shapes=[
            pltpu.VMEM((2, modes, modes), BF16),
            pltpu.VMEM((modes, modes), BF16),
            pltpu.VMEM((steps, cols, modes), BF16),
            pltpu.VMEM((cols, modes), BF16),
            pltpu.VMEM((steps, cols, modes), BF16),
            pltpu.VMEM((cols, modes), F32),
            pltpu.VMEM((cols, modes), F32),
            pltpu.VMEM((cols, modes), F32),
            pltpu.VMEM((cols, modes), F32),
            pltpu.VMEM((steps, cols, modes), F32),
            pltpu.VMEM((steps, cols, modes), F32),
            pltpu.VMEM((times_n, cols, modes), F32),
            pltpu.VMEM((times_n, cols, modes), F32),
            pltpu.VMEM((cols, modes), F32),
            dma((8,)),
            dma((5 * (modes_n - 1),)),
            dma((5 * (modes_n - 1),)),
            dma((2,)),
            dma((2,)),
            dma((count,)),
            dma((count,)),
            dma((count,)),
            dma((count,)),
            dma((count,)),
            dma((count,)),
            dma((count,)),
            dma((count,)),
            pltpu.SemaphoreType.REGULAR((max(1, times_n - 2),)),
            pltpu.SemaphoreType.REGULAR((max(1, times_n - 2),)),
            dma((times_n - 1,)),
            dma((times_n,)),
            dma((times_n - 1,)),
            dma((times_n,)),
        ],
        compiler_params=pltpu.CompilerParams(
            collective_id=0, has_side_effects=True, vmem_limit_bytes=60 * 1024 * 1024
        ),
    )(flags, base, solar, target, state, adjoint, sun, eclipse, coarse)


def solution(mesh):
    cells = P(("group", "tm"), "col", "mode")
    in_specs = (
        P(("group", "tm")),
        cells,
        P(("group", "col"), "mode"),
        cells,
        cells,
        cells,
        P("mode", None),
        P("mode", None),
        P("mode", None),
    )
    call = functools.partial(local, mesh.shape["mode"], mesh.shape["tm"])
    return jax.shard_map(call, mesh=mesh, in_specs=in_specs, out_specs=(cells, cells), check_vma=False)
```

```python
import functools

import jax
import jax.numpy as jnp
from jax import lax
from jax.experimental import pallas as pl
from jax.experimental.pallas import tpu as pltpu
from jax.sharding import PartitionSpec as P

OBJ_WEIGHT = 0.0625
MESH = pl.DeviceIdType.MESH
BF16 = jnp.bfloat16
F32 = jnp.float32
TILE = 256
NT_DIMS = (((1,), (1,)), ((), ()))
NN_DIMS = (((1,), (0,)), ((), ()))


def remote(src, dst, send, recv, **where):
    return pltpu.make_async_remote_copy(
        src_ref=src, dst_ref=dst, send_sem=send, recv_sem=recv, device_id=where, device_id_type=MESH
    )


def times_transposed(rows, tile_of, modes):
    parts = []
    for j in range(modes // TILE):
        tile = tile_of(pl.ds(j * TILE, TILE), slice(None))
        parts.append(lax.dot_general(rows, tile, NT_DIMS, preferred_element_type=F32))
    return jnp.concatenate(parts, axis=1)


def times_plain(rows, tile_of, modes):
    parts = []
    for j in range(modes // TILE):
        tile = tile_of(slice(None), pl.ds(j * TILE, TILE))
        parts.append(lax.dot_general(rows, tile, NN_DIMS, preferred_element_type=F32))
    return jnp.concatenate(parts, axis=1)


def pieces(value):
    hi = value.astype(BF16)
    rest = value - hi.astype(F32)
    mid = rest.astype(BF16)
    lo = (rest - mid.astype(F32)).astype(BF16)
    return jnp.concatenate([hi, mid, lo], axis=0)


def collect(product, cols):
    return product[:cols] + product[cols : 2 * cols] + product[2 * cols :]


def kernel(
    modes_n,
    times_n,
    chunks,
    flags,
    base,
    solar,
    target,
    state,
    adjoint,
    sun,
    eclipse,
    coarse,
    both_out,
    mats,
    cmat,
    base_f,
    solar_f,
    target_f,
    state_f,
    adj_f,
    state_next,
    adj_next,
    traj,
    path,
    res_f,
    res_b,
    corr,
    own_sem,
    small_send,
    small_recv,
    next_send,
    next_recv,
    one_send,
    one_recv,
    y_send,
    y_recv,
    c_send,
    c_recv,
    d_send,
    d_recv,
    far_low,
    far_high,
    rf_send,
    rf_recv,
    rb_send,
    rb_recv,
):
    g = lax.axis_index("group")
    t = lax.axis_index("tm")
    m = lax.axis_index("mode")
    c = lax.axis_index("col")
    rows = sun.shape[0]
    modes = sun.shape[1]
    steps, cols = base.shape[0], base.shape[1]
    quarter = rows // 4
    piece = quarter // chunks
    mate = 1 - c
    twin = 1 - g

    def lanes(index):
        return pl.ds(pl.multiple_of(index * rows, 128), rows)

    mine = lanes(m)

    own = [
        (state.at[0], state_f.at[:, mine]),
        (base, base_f.at[:, :, mine]),
        (solar, solar_f.at[:, mine]),
        (sun, mats.at[0, pl.ds(pl.multiple_of(m * rows, 16), rows), :]),
        (eclipse, mats.at[1, pl.ds(pl.multiple_of(m * rows, 16), rows), :]),
        (target, target_f.at[:, :, mine]),
        (adjoint.at[0], adj_f.at[:, mine]),
        (coarse, cmat.at[pl.ds(pl.multiple_of(m * rows, 16), rows), :]),
    ]
    own_copies = [pltpu.make_async_copy(s, d, own_sem.at[i]) for i, (s, d) in enumerate(own)]
    for copy in own_copies:
        copy.start()

    barrier = pltpu.get_barrier_semaphore()
    pl.semaphore_signal(barrier, inc=1, device_id={"col": mate}, device_id_type=MESH)
    pl.semaphore_signal(barrier, inc=1, device_id={"group": twin}, device_id_type=MESH)
    for d in range(1, modes_n):
        pl.semaphore_signal(barrier, inc=1, device_id={"mode": lax.rem(m + d, modes_n)}, device_id_type=MESH)

    def signal_tm(semaphore, where):
        pl.semaphore_signal(semaphore, inc=1, device_id={"tm": where}, device_id_type=MESH)

    @pl.when(t > 0)
    def _():
        signal_tm(barrier, t - 1)

    @pl.when(t < times_n - 1)
    def _():
        signal_tm(barrier, t + 1)

    has_low = lax.div(t + times_n - 1, times_n)
    has_high = lax.div(2 * times_n - 2 - t, times_n)
    pl.semaphore_wait(barrier, modes_n + 1 + has_low + has_high)

    def pass_on(entry):
        @pl.when(jnp.logical_and(t - 1 - entry >= 0, t + 1 < times_n))
        def _():
            signal_tm(far_low.at[entry], t + 1)

        @pl.when(jnp.logical_and(t + 1 + entry < times_n, t - 1 >= 0))
        def _():
            signal_tm(far_high.at[entry], t - 1)

    def hear(entry):
        @pl.when(t - 2 - entry >= 0)
        def _():
            pl.semaphore_wait(far_low.at[entry], 1)

        @pl.when(t + 2 + entry < times_n)
        def _():
            pl.semaphore_wait(far_high.at[entry], 1)

    def peer(d):
        return lax.rem(m + d, modes_n)

    def source(d):
        return lax.rem(m + modes_n - d, modes_n)

    small_srcs = [state.at[0], base, solar, target, adjoint.at[0]]

    def small_dst(kind, where):
        if kind == 0:
            return state_f.at[:, where]
        if kind == 1:
            return base_f.at[:, :, where]
        if kind == 2:
            return solar_f.at[:, where]
        if kind == 3:
            return target_f.at[:, :, where]
        return adj_f.at[:, where]

    def small(kind, d):
        at = kind * (modes_n - 1) + d - 1
        return remote(
            small_srcs[kind], small_dst(kind, mine), small_send.at[at], small_recv.at[at], mode=peer(d)
        )

    mat_srcs = [sun, eclipse, coarse]

    def mat_rows(k, start):
        where = pl.ds(pl.multiple_of(start, 16), piece)
        if k < 2:
            return mats.at[k, where, :]
        return cmat.at[where, :]

    order = []
    for k in range(3):
        for q in range(chunks):
            for d in range(1, modes_n):
                order.append((k, q, d))

    part = (g * 2 + c) * quarter
    twin_part = (twin * 2 + c) * quarter

    def first(at):
        k, q, d = order[at]
        inside = part + q * piece
        return remote(
            mat_srcs[k].at[pl.ds(pl.multiple_of(inside, 16), piece), :],
            mat_rows(k, m * rows + inside),
            one_send.at[at],
            one_recv.at[at],
            mode=peer(d),
        )

    def arrived_rows(at, owner_part):
        k, q, d = order[at]
        return mat_rows(k, source(d) * rows + owner_part + q * piece)

    def to_twin(at):
        ref = arrived_rows(at, part)
        return remote(ref, ref, y_send.at[at], y_recv.at[at], group=twin)

    def to_mate(at):
        ref = arrived_rows(at, part)
        return remote(ref, ref, c_send.at[at], c_recv.at[at], col=mate)

    def twin_to_mate(at):
        ref = arrived_rows(at, twin_part)
        return remote(ref, ref, d_send.at[at], d_recv.at[at], col=mate)

    per_mat = chunks * (modes_n - 1)

    def start_small(kinds):
        for kind in kinds:
            for d in range(1, modes_n):
                small(kind, d).start()

    for at in range(2 * per_mat):
        first(at).start()
    start_small((0, 1, 2))
    start_small((4, 3))
    for at in range(2 * per_mat, 3 * per_mat):
        first(at).start()

    if times_n > 2:
        pass_on(0)

    def wait_small(kind):
        for d in range(1, modes_n):
            small(kind, d).wait_recv()

    back_down = lax.rem(t + times_n - 1, times_n)

    def next_copy(index):
        src, dst = ((state_f, state_next), (adj_f, adj_next))[index]
        return remote(src, dst, next_send.at[index], next_recv.at[index], tm=back_down)

    def relay(first_at, last_at):
        for at in range(first_at, last_at + 1):
            if at < last_at:
                first(at).wait_recv()
                to_twin(at).start()
                to_mate(at).start()
            if at > first_at:
                to_twin(at - 1).wait_recv()
                twin_to_mate(at - 1).start()

    def settle(first_at, last_at):
        for at in range(first_at, last_at):
            to_mate(at).wait_recv()
            twin_to_mate(at).wait_recv()

    relay(0, 2 * per_mat)
    own_copies[0].wait()
    wait_small(0)

    @pl.when(t > 0)
    def _():
        next_copy(0).start()

    for index in (1, 2, 3, 4):
        own_copies[index].wait()
    wait_small(1)
    wait_small(2)
    settle(0, 2 * per_mat)

    def forcing(n):
        sun_on = (1 - flags[n]).astype(F32)
        return base_f[n].astype(F32) + sun_on * solar_f[...].astype(F32)

    def forward(n, w):
        flag = flags[n]
        return times_transposed(w.astype(BF16), lambda a, b: mats[flag, a, b], modes) + forcing(n)

    ends = lax.fori_loop(0, steps, forward, state_f[...])

    @pl.when(t < times_n - 1)
    def _():
        next_copy(0).wait_recv()
        res_f[t + 1] = ends - state_next[...]

    for entry in range(times_n - 2):
        hear(entry)
        if entry + 1 < times_n - 2:
            pass_on(entry + 1)

    def res_copy(k):
        slot = lax.rem(t + 1, times_n)
        return remote(
            res_f.at[slot], res_f.at[slot], rf_send.at[k - 1], rf_recv.at[slot], tm=lax.rem(t + k, times_n)
        )

    for k in range(times_n - 1, 0, -1):

        @pl.when(t + k < times_n)
        def _():
            res_copy(k).start()

    own_copies[6].wait()
    wait_small(4)

    @pl.when(t > 0)
    def _():
        next_copy(1).start()

    relay(2 * per_mat, 3 * per_mat)
    own_copies[5].wait()
    own_copies[7].wait()
    wait_small(3)
    settle(2 * per_mat, 3 * per_mat)

    def wait_res(j):
        remote(res_f.at[j], res_f.at[j], rf_send.at[0], rf_recv.at[j], tm=t).wait_recv()

    corr[...] = jnp.zeros_like(corr)

    @pl.when(t >= 1)
    def _():
        wait_res(1)
        corr[...] = res_f[1]

    def coarse_up(j, carry):
        wait_res(j)
        product = times_transposed(pieces(corr[...]), lambda a, b: cmat[a, b], modes)
        corr[...] = collect(product, cols) + res_f[j]
        return carry

    lax.fori_loop(2, t + 1, coarse_up, 0)

    corrected = state_f[...] + corr[...]
    traj[0] = corrected

    def forward_keep(n, w):
        w = forward(n, w)
        traj[n + 1] = w
        return w

    lax.fori_loop(0, steps - 1, forward_keep, corrected)

    def backward(n, w):
        flag = flags[n]
        product = times_plain(w.astype(BF16), lambda a, b: mats[flag, a, b], modes)
        return product + OBJ_WEIGHT * (traj[n] - target_f[n].astype(F32))

    @pl.when(t < times_n - 1)
    def _():
        next_copy(1).wait_recv()

    @pl.when(t == times_n - 1)
    def _():
        adj_next[...] = jnp.zeros_like(adj_next)

    back = lax.fori_loop(0, steps, lambda i, w: backward(steps - 1 - i, w), adj_next[...])
    res_b[t] = back - adj_f[...]

    def back_copy(k):
        return remote(res_b.at[t], res_b.at[t], rb_send.at[k - 1], rb_recv.at[t], tm=lax.rem(t + times_n - k, times_n))

    for k in range(times_n - 1, 0, -1):

        @pl.when(t - k >= 0)
        def _():
            back_copy(k).start()

    both_out[0] = traj[:, :, mine]

    def wait_back(j):
        remote(res_b.at[j], res_b.at[j], rb_send.at[0], rb_recv.at[j], tm=t).wait_recv()

    @pl.when(t < times_n - 1)
    def _():
        wait_back(times_n - 1)

    corr[...] = res_b[times_n - 1]

    def coarse_down(i, carry):
        j = times_n - 2 - i
        wait_back(j)
        product = times_plain(pieces(corr[...]), lambda a, b: cmat[a, b], modes)
        corr[...] = collect(product, cols) + res_b[j]
        return carry

    lax.fori_loop(0, times_n - 2 - t, coarse_down, 0)

    @pl.when(t < times_n - 1)
    def _():
        later = corr[...]
        adj_next[...] = adj_next[...] + later
        product = times_plain(pieces(later), lambda a, b: cmat[a, b], modes)
        corr[...] = collect(product, cols) + res_b[t]

    path[0] = adj_f[...] + corr[...]

    def backward_keep(i, w):
        n = steps - 1 - i
        w = backward(n, w)
        path[n] = w
        return w

    lax.fori_loop(0, steps - 1, backward_keep, adj_next[...])
    both_out[1] = path[:, :, mine]

    for kind in range(5):
        for d in range(1, modes_n):
            small(kind, d).wait_send()
    for at in range(3 * per_mat):
        first(at).wait_send()
        to_twin(at).wait_send()
        to_mate(at).wait_send()
        twin_to_mate(at).wait_send()

    @pl.when(t > 0)
    def _():
        next_copy(0).wait_send()
        next_copy(1).wait_send()

    for k in range(times_n - 1, 0, -1):

        @pl.when(t + k < times_n)
        def _():
            res_copy(k).wait_send()

        @pl.when(t - k >= 0)
        def _():
            back_copy(k).wait_send()


def local(modes_n, times_n, flags, base, solar, target, state, adjoint, sun, eclipse, coarse):
    rows, modes = sun.shape
    steps, cols = base.shape[0], base.shape[1]
    chunks = max(1, min(2, rows // 4 // 32))
    count = 3 * chunks * (modes_n - 1)
    dma = pltpu.SemaphoreType.DMA
    hbm = pl.BlockSpec(memory_space=pl.ANY)
    vmem = pl.BlockSpec(memory_space=pltpu.VMEM)
    outs = jax.ShapeDtypeStruct((2, steps, cols, rows), F32)
    both = pl.pallas_call(
        functools.partial(kernel, modes_n, times_n, chunks),
        out_shape=outs,
        in_specs=[pl.BlockSpec(memory_space=pltpu.SMEM)] + [hbm] * 8,
        out_specs=vmem,
        scratch_shapes=[
            pltpu.VMEM((2, modes, modes), BF16),
            pltpu.VMEM((modes, modes), BF16),
            pltpu.VMEM((steps, cols, modes), BF16),
            pltpu.VMEM((cols, modes), BF16),
            pltpu.VMEM((steps, cols, modes), BF16),
            pltpu.VMEM((cols, modes), F32),
            pltpu.VMEM((cols, modes), F32),
            pltpu.VMEM((cols, modes), F32),
            pltpu.VMEM((cols, modes), F32),
            pltpu.VMEM((steps, cols, modes), F32),
            pltpu.VMEM((steps, cols, modes), F32),
            pltpu.VMEM((times_n, cols, modes), F32),
            pltpu.VMEM((times_n, cols, modes), F32),
            pltpu.VMEM((cols, modes), F32),
            dma((8,)),
            dma((5 * (modes_n - 1),)),
            dma((5 * (modes_n - 1),)),
            dma((2,)),
            dma((2,)),
            dma((count,)),
            dma((count,)),
            dma((count,)),
            dma((count,)),
            dma((count,)),
            dma((count,)),
            dma((count,)),
            dma((count,)),
            pltpu.SemaphoreType.REGULAR((max(1, times_n - 2),)),
            pltpu.SemaphoreType.REGULAR((max(1, times_n - 2),)),
            dma((times_n - 1,)),
            dma((times_n,)),
            dma((times_n - 1,)),
            dma((times_n,)),
        ],
        compiler_params=pltpu.CompilerParams(
            collective_id=0, has_side_effects=True, vmem_limit_bytes=60 * 1024 * 1024
        ),
    )(flags, base, solar, target, state, adjoint, sun, eclipse, coarse)
    return both[0], both[1]


def solution(mesh):
    cells = P(("group", "tm"), "col", "mode")
    in_specs = (
        P(("group", "tm")),
        cells,
        P(("group", "col"), "mode"),
        cells,
        cells,
        cells,
        P("mode", None),
        P("mode", None),
        P("mode", None),
    )
    call = functools.partial(local, mesh.shape["mode"], mesh.shape["tm"])
    return jax.shard_map(call, mesh=mesh, in_specs=in_specs, out_specs=(cells, cells), check_vma=False)
```
